32 devices in a mesh: parts: 2 (over y), design: 4 (over z), dap: 4 (over x, core).
Axes of the slice: x: 2, y: 2, z: 4, core: 2. Of those that a mesh axis runs over, the one named last changes fastest.
Arguments:
- pair: bfloat16 [8, 256, 256, 128], P(('parts', 'design'), 'dap'), parts along dimension 0, may hold values from -6 to 6
- lengths: int32 [8], P(('parts', 'design')), parts along dimension 0, may hold values from 64 to 256, as said below
- attn_gain: float32 [2, 128], replicated, may hold values from 0.1 to 1.9
- attn_proj: bfloat16 [2, 128, 512], replicated, may hold values from -0.5 to 0.5
- attn_bias: bfloat16 [2, 128, 4], replicated, may hold values from -0.5 to 0.5
- attn_out: bfloat16 [2, 128, 128], replicated, may hold values from -0.5 to 0.5
- trans_gain: float32 [128], replicated, may hold values from 0.1 to 1.9
- trans_up: bfloat16 [128, 512], replicated, may hold values from -0.5 to 0.5
- trans_down: bfloat16 [512, 128], replicated, may hold values from -0.25 to 0.25
Outputs:
- updated: bfloat16 [8, 256, 256, 128], P(('parts', 'design'), 'dap'), parts along dimension 0
The draws below stay inside these ranges and needn't reach their ends.
There are 2 independent parts, one for each index of `parts`. The reference program is written for one: setup_inputs(seed, part) draws one part's arguments, and reference() takes and returns one part's arrays. A program takes and returns all parts, laid end to end along the dimension named above; an argument that names none is the same for every part. Nothing has to cross between parts.
Inputs may be any that keep to these rules, and one draw needn't show every extreme that they name: `lengths`: some protein of every group has exactly 256 residues.
All inputs are finite; a program needn't handle non-finite values.
Results may differ from the reference program's by a relative error of at most 0.008.
Values may be sent and summed in bfloat16 or wider, within the bound.
A program may use at most 128 MiB of HBM per device.

```python
import math
import jax
import jax.numpy as jnp
from jax import lax

C = 128
H = 4
HD = 32
LMAX = 256
TRANS = 512
PROTEINS = 4


def draw_lengths(key, part):
    key = jax.random.fold_in(key, 11)
    base = jax.random.randint(jax.random.fold_in(key, 1), (PROTEINS,), LMAX // 4, LMAX + 1)
    chosen = jax.random.randint(jax.random.fold_in(key, 2), (), 0, PROTEINS)
    places = jnp.arange(PROTEINS, dtype=jnp.int32)
    return jnp.where(places == chosen, LMAX, base).astype(jnp.int32)


def levels(key, shape, pieces, low, top_value):
    def one(dim, shards_of):
        heights = jax.random.uniform(jax.random.fold_in(jax.random.fold_in(key, 6), dim), (shards_of,), jnp.float32, low / len(pieces), top_value / len(pieces))
        return jnp.repeat(jnp.exp(heights), shape[dim] // shards_of).reshape((-1,) + (1,) * (len(shape) - dim - 1))

    level = one(*pieces[0])
    for cut in pieces[1:]:
        level = level * one(*cut)
    return level


def centred(own_key, shape, deviation, reach, split=(), kind=jnp.bfloat16):
    level = levels(own_key, shape, split, -0.22, 0.18) if split else 1.0
    values = jax.random.normal(own_key, shape, jnp.float32) * deviation * level
    return jnp.minimum(jnp.maximum(values, -reach), reach).astype(kind)


def setup_inputs(seed: int = 0, part: int = 0) -> dict:
    keys = jax.random.split(jax.random.key(seed), 10)
    part_keys = jax.random.split(jax.random.fold_in(keys[9], part), 10)
    return {
        "pair": centred(part_keys[0], (PROTEINS, LMAX, LMAX, C), 1.0, 6.0, ((0, 4), (1, 4))),
        "lengths": draw_lengths(jax.random.fold_in(jax.random.fold_in(keys[9], part), 71), part),
        "attn_gain": jnp.clip(1.0 + 0.18 * jax.random.normal(keys[2], (2, C), jnp.float32), 0.1, 1.9),
        "attn_proj": centred(keys[3], (2, C, 4 * H * HD), C ** -0.5, 0.5),
        "attn_bias": centred(keys[4], (2, C, H), C ** -0.5, 0.5),
        "attn_out": centred(keys[5], (2, H * HD, C), (H * HD) ** -0.5, 0.5),
        "trans_gain": jnp.clip(1.0 + 0.18 * jax.random.normal(keys[6], (C,), jnp.float32), 0.1, 1.9),
        "trans_up": centred(keys[7], (C, TRANS), C ** -0.5, 0.5),
        "trans_down": centred(keys[8], (TRANS, C), TRANS ** -0.5, 0.25),
    }


EPSILON = 1e-05

def layer_norm(values, gain):
    values = values.astype(jnp.float32)
    center = values - lax.optimization_barrier(jnp.mean(values, axis=-1, keepdims=True))
    spread = lax.optimization_barrier(jnp.mean(center * center, axis=-1, keepdims=True))
    return center * lax.rsqrt(spread + EPSILON) * gain

def attend_rows(pair_rows, normed, bias_full, live_keys, w_proj, w_out):
    rows, extent, width = pair_rows.shape
    heads = bias_full.shape[0]
    head_size = w_out.shape[0] // heads
    projected = jnp.dot(normed, w_proj, preferred_element_type=jnp.float32).astype(jnp.bfloat16)
    projected = projected.reshape(rows, extent, 4, heads, head_size)
    factor = 1.0 / math.sqrt(head_size)
    bias_wide = bias_full.astype(jnp.float32)

    def one_row(single):
        query = single[:, 0].astype(jnp.float32)
        keyed = single[:, 1].astype(jnp.float32)
        valued = single[:, 2].astype(jnp.float32)
        logits = jnp.einsum('jhd,khd->hjk', query, keyed) * factor + bias_wide
        logits = jnp.where(live_keys[None, None, :], logits, -1000000000.0)
        probs = jax.nn.softmax(logits, axis=-1).astype(jnp.bfloat16)
        mixed = jnp.einsum('hjk,khd->jhd', probs.astype(jnp.float32), valued)
        gated = (mixed * jax.nn.sigmoid(single[:, 3].astype(jnp.float32))).astype(jnp.bfloat16)
        return gated.reshape(extent, heads * head_size)
    gated = lax.map(one_row, projected)
    update = jnp.dot(gated, w_out, preferred_element_type=jnp.float32)
    return (pair_rows.astype(jnp.float32) + update).astype(jnp.bfloat16)

def transition(pair_rows, gain, w_up, w_down):
    normed = layer_norm(pair_rows, gain).astype(jnp.bfloat16)
    hidden = jax.nn.relu(jnp.dot(normed, w_up, preferred_element_type=jnp.float32)).astype(jnp.bfloat16)
    out_term = jnp.dot(hidden, w_down, preferred_element_type=jnp.float32)
    return (pair_rows.astype(jnp.float32) + out_term).astype(jnp.bfloat16)

def make_bias(normed, w_bias):
    return jnp.einsum('jkc,ch->hjk', normed.astype(jnp.float32), w_bias.astype(jnp.float32)).astype(jnp.bfloat16)

def one_protein(single_pair, length, attn_gain, attn_proj, attn_bias, attn_out, trans_gain, trans_up, trans_down):
    extent = single_pair.shape[0]
    live_keys = jnp.arange(extent, dtype=jnp.int32) < length
    normed = layer_norm(single_pair, attn_gain[0]).astype(jnp.bfloat16)
    first = attend_rows(single_pair, normed, make_bias(normed, attn_bias[0]), live_keys, attn_proj[0], attn_out[0])
    flipped = jnp.swapaxes(first, 0, 1)
    normed = layer_norm(flipped, attn_gain[1]).astype(jnp.bfloat16)
    second = attend_rows(flipped, normed, make_bias(normed, attn_bias[1]), live_keys, attn_proj[1], attn_out[1])
    third = transition(second, trans_gain, trans_up, trans_down)
    back = jnp.swapaxes(third, 0, 1)
    keep = live_keys[:, None] & live_keys[None, :]
    return jnp.where(keep[:, :, None], back, jnp.zeros_like(back)).astype(jnp.bfloat16)

def reference(pair, lengths, attn_gain, attn_proj, attn_bias, attn_out, trans_gain, trans_up, trans_down):

    def per_item(item):
        return one_protein(item[0], item[1], attn_gain, attn_proj, attn_bias, attn_out, trans_gain, trans_up, trans_down)
    return lax.map(per_item, (pair, lengths))
```

```python
import functools
import math

import jax
import jax.numpy as jnp
from jax import lax
from jax.experimental import pallas as pl
from jax.experimental.pallas import tpu as pltpu
from jax.sharding import PartitionSpec as P

EPSILON = 1e-05
LOG2E = math.log2(math.e)
TILE = 16
UNROLL = 2
BF16 = jnp.bfloat16
F32 = jnp.float32
MESH = pl.DeviceIdType.MESH


def layer_norm(values, gain):
    center = values - jnp.mean(values, axis=-1, keepdims=True)
    spread = jnp.mean(center * center, axis=-1, keepdims=True)
    return (center * lax.rsqrt(spread + EPSILON) * gain).astype(BF16)


def dot_nt(left, right):
    return lax.dot_general(left, right, (((1,), (1,)), ((), ())), preferred_element_type=F32)


def dot_nn(left, right):
    return jnp.dot(left, right, preferred_element_type=F32)


def kernel(
    groups,
    heads,
    pair_ref,
    len_ref,
    gain_ref,
    proj_ref,
    wbias_ref,
    wout_ref,
    tgain_ref,
    up_ref,
    down_ref,
    out_ref,
    norm_ref,
    x2_ref,
    stage1,
    stage2,
    brow,
    bsend1,
    bsend2,
    bfull1,
    bfull2,
    bias_ref,
    turn,
    bias_send,
    bias_recv,
    one_send,
    one_recv,
    two_send,
    two_recv,
    own_sem,
):
    rows, extent, width = pair_ref.shape
    head_size = width // heads
    blocks = rows // TILE
    me = lax.axis_index("dap")
    length = len_ref[0]
    first_row = pl.multiple_of(me * rows, TILE)

    def peer(offset):
        return lax.rem(me + offset, groups)

    barrier = pltpu.get_barrier_semaphore()
    for offset in range(1, groups):
        pl.semaphore_signal(barrier, inc=1, device_id={"dap": peer(offset)}, device_id_type=MESH)
    pl.semaphore_wait(barrier, groups - 1)

    lane_head = lax.broadcasted_iota(jnp.int32, (1, width), 1) // head_size
    head_masks = [(lane_head == h).astype(F32).astype(BF16) for h in range(heads)]

    def bias_rows(index, normed, which):
        values = dot_nt(wbias_ref[which], normed)
        for part in range(extent // 128):
            half = values[:8, part * 128 : (part + 1) * 128]
            brow[part, pl.ds(pl.multiple_of(index * 8, 8), 8), :] = half

    def bias_copy(offset, which):
        src = (bsend1, bsend2)[which]
        dst = (bfull1, bfull2)[which]
        return pltpu.make_async_remote_copy(
            src_ref=src,
            dst_ref=dst.at[:, pl.ds(first_row, rows), :],
            send_sem=bias_send.at[which, offset],
            recv_sem=bias_recv.at[which, offset],
            device_id={"dap": peer(offset)},
            device_id_type=MESH,
        )

    def bias_start(which):
        src = (bsend1, bsend2)[which]
        dst = (bfull1, bfull2)[which]
        for h in range(heads):
            halves = [brow[part, pl.ds(h, rows, stride=8), :] for part in range(extent // 128)]
            piece = jnp.concatenate(halves, axis=1).astype(BF16)
            src[h] = piece
            dst[h, pl.ds(first_row, rows), :] = piece
        for offset in range(1, groups):
            bias_copy(offset, which).start()

    def bias_finish(which):
        for offset in range(1, groups):
            bias_copy(offset, which).wait()
        dst = (bfull1, bfull2)[which]
        live = lax.broadcasted_iota(jnp.int32, (1, extent), 1) < length
        for h in range(heads):
            wide = dst[h].astype(F32)
            if which == 1:
                wide = wide.T
            bias_ref[h] = jnp.where(live, wide * LOG2E, -1000000000.0)

    def attend(x, normed, which):
        projected = dot_nn(normed, proj_ref[which])
        factor = LOG2E / math.sqrt(head_size)
        query = (projected[:, :width] * factor).astype(BF16)
        keyed = projected[:, width : 2 * width].astype(BF16)
        valued = projected[:, 2 * width : 3 * width].astype(BF16)
        gate = projected[:, 3 * width :]
        probs = []
        wide_values = []
        for h in range(heads):
            logits = dot_nt(query, keyed * head_masks[h]) + bias_ref[h]
            top = jnp.max(logits, axis=-1, keepdims=True)
            probs.append(jnp.exp2(logits - top).astype(BF16))
            ones = jnp.broadcast_to(head_masks[h], (extent, width))
            wide_values.append(jnp.concatenate([valued * head_masks[h], ones], axis=1))
        mixed = dot_nn(jnp.concatenate(probs, axis=1), jnp.concatenate(wide_values, axis=0))
        gated = mixed[:, :width] / (mixed[:, width:] * (1.0 + jnp.exp(-gate)))
        return x + dot_nn(gated.astype(BF16), wout_ref[which])

    def transition(x):
        hidden = jnp.maximum(dot_nn(layer_norm(x, tgain_ref[...]), up_ref[...]), 0.0)
        return x + dot_nn(hidden.astype(BF16), down_ref[...])

    def piece_copy(block, offset, phase):
        to = pl.multiple_of(peer(offset) * rows, TILE)
        src = (stage1, stage2)[phase]
        dst = (x2_ref, out_ref)[phase]
        local = src.at[pl.ds(to, rows), pl.ds(pl.multiple_of(block * TILE, TILE), TILE), :]
        place = dst.at[:, pl.ds(pl.multiple_of(first_row + block * TILE, TILE), TILE), :]
        if offset == 0:
            return pltpu.make_async_copy(local, place, own_sem.at[phase, block])
        return pltpu.make_async_remote_copy(
            src_ref=local,
            dst_ref=place,
            send_sem=(one_send, two_send)[phase].at[block, offset],
            recv_sem=(one_recv, two_recv)[phase].at[block, offset],
            device_id={"dap": peer(offset)},
            device_id_type=MESH,
        )

    def send_block(block, phase):
        stage = (stage1, stage2)[phase]
        turned = turn[...].reshape(extent, TILE, width).astype(BF16)
        stage[:, pl.ds(pl.multiple_of(block * TILE, TILE), TILE), :] = turned
        for offset in list(range(1, groups)) + [0]:
            piece_copy(block, offset, phase).start()

    def finish_blocks(phase):
        def body(block, carry):
            for offset in range(groups):
                piece_copy(block, offset, phase).wait()
            return carry

        lax.fori_loop(0, blocks, body, 0)

    def bias_body(step, carry):
        for part in range(UNROLL):
            index = step * UNROLL + part
            normed = layer_norm(pair_ref[index].astype(F32), gain_ref[0:1])
            norm_ref[index] = normed
            bias_rows(index, normed, 0)
        return carry

    lax.fori_loop(0, rows // UNROLL, bias_body, 0)
    bias_start(0)
    bias_finish(0)

    def one_block(block, carry):
        def one_body(step, inner):
            for part in range(UNROLL):
                local = step * UNROLL + part
                index = block * TILE + local
                first = attend(pair_ref[index].astype(F32), norm_ref[index], 0)
                turn[pl.ds(local, extent, stride=TILE), :] = first
                rounded = first.astype(BF16).astype(F32)
                bias_rows(index, layer_norm(rounded, gain_ref[1:2]), 1)
            return inner

        lax.fori_loop(0, TILE // UNROLL, one_body, 0)
        send_block(block, 0)
        return carry

    lax.fori_loop(0, blocks, one_block, 0)
    bias_start(1)
    finish_blocks(0)
    bias_finish(1)

    row_live = lax.broadcasted_iota(jnp.int32, (extent, width), 0) < length

    def two_block(block, carry):
        def two_body(step, inner):
            for part in range(UNROLL):
                local = step * UNROLL + part
                index = block * TILE + local
                x = x2_ref[index].astype(F32)
                second = attend(x, layer_norm(x, gain_ref[1:2]), 1)
                third = transition(second.astype(BF16).astype(F32))
                limit = jnp.where(first_row + index < length, 1.0, 0.0)
                turn[pl.ds(local, extent, stride=TILE), :] = jnp.where(row_live, third * limit, 0.0)
            return inner

        lax.fori_loop(0, TILE // UNROLL, two_body, 0)
        send_block(block, 1)
        return carry

    lax.fori_loop(0, blocks, two_block, 0)
    finish_blocks(1)


def on_device(
    pair, lengths, attn_gain, attn_proj, attn_bias, attn_out, trans_gain, trans_up, trans_down
):
    current = pair[0]
    rows, extent, width = current.shape
    heads = attn_bias.shape[2]
    groups = lax.axis_size("dap")
    blocks = rows // TILE
    wbias = jnp.pad(jnp.swapaxes(attn_bias, 1, 2), ((0, 0), (0, 16 - heads), (0, 0)))
    vmem = pl.BlockSpec(memory_space=pltpu.VMEM)
    dma = pltpu.SemaphoreType.DMA
    result = pl.pallas_call(
        functools.partial(kernel, groups, heads),
        out_shape=jax.ShapeDtypeStruct(current.shape, BF16),
        in_specs=[vmem, pl.BlockSpec(memory_space=pltpu.SMEM)] + [vmem] * 7,
        out_specs=pl.BlockSpec(memory_space=pl.ANY),
        scratch_shapes=[
            pltpu.VMEM((rows, extent, width), BF16),
            pltpu.VMEM((rows, extent, width), BF16),
            pltpu.VMEM((extent, rows, width), BF16),
            pltpu.VMEM((extent, rows, width), BF16),
            pltpu.VMEM((extent // 128, rows * 8, 128), F32),
            pltpu.VMEM((heads, rows, extent), BF16),
            pltpu.VMEM((heads, rows, extent), BF16),
            pltpu.VMEM((heads, extent, extent), BF16),
            pltpu.VMEM((heads, extent, extent), BF16),
            pltpu.VMEM((heads, extent, extent), F32),
            pltpu.VMEM((extent * TILE, width), F32),
            dma((2, groups)),
            dma((2, groups)),
            dma((blocks, groups)),
            dma((blocks, groups)),
            dma((blocks, groups)),
            dma((blocks, groups)),
            dma((2, blocks)),
        ],
        compiler_params=pltpu.CompilerParams(
            collective_id=0, has_side_effects=True, vmem_limit_bytes=56 * 1024 * 1024
        ),
        cost_estimate=pl.CostEstimate(
            flops=20 * 1000**3, bytes_accessed=16 * 1000**2, transcendentals=40 * 1000**2
        ),
    )(current, lengths, attn_gain, attn_proj, wbias, attn_out, trans_gain[None], trans_up, trans_down)
    return result[None]


def solution(mesh):
    in_specs = (
        P(("parts", "design"), "dap", None, None),
        P(("parts", "design")),
        P(),
        P(),
        P(),
        P(),
        P(),
        P(),
        P(),
    )
    out_specs = P(("parts", "design"), "dap", None, None)
    return jax.shard_map(
        on_device, mesh=mesh, in_specs=in_specs, out_specs=out_specs, check_vma=False
    )
```

```python
import functools
import math

import jax
import jax.numpy as jnp
from jax import lax
from jax.experimental import pallas as pl
from jax.experimental.pallas import tpu as pltpu
from jax.sharding import PartitionSpec as P

EPSILON = 1e-05
LOG2E = math.log2(math.e)
TILE = 16
UNROLL = 4
BF16 = jnp.bfloat16
F32 = jnp.float32
MESH = pl.DeviceIdType.MESH


def layer_norm(values, gain):
    center = values - jnp.mean(values, axis=-1, keepdims=True)
    spread = jnp.mean(center * center, axis=-1, keepdims=True)
    return (center * lax.rsqrt(spread + EPSILON) * gain).astype(BF16)


def dot_nt(left, right):
    return lax.dot_general(left, right, (((1,), (1,)), ((), ())), preferred_element_type=F32)


def dot_nn(left, right):
    return jnp.dot(left, right, preferred_element_type=F32)


def kernel(
    groups,
    heads,
    pair_ref,
    len_ref,
    gain_ref,
    proj_ref,
    wbias_ref,
    wout_ref,
    tgain_ref,
    up_ref,
    down_ref,
    out_ref,
    norm_ref,
    x2_ref,
    stage1,
    stage2,
    brow,
    bsend1,
    bsend2,
    bfull1,
    bfull2,
    bias_ref,
    turn,
    bias_send,
    bias_recv,
    one_send,
    one_recv,
    two_send,
    two_recv,
    own_sem,
):
    rows, extent, width = pair_ref.shape
    head_size = width // heads
    blocks = rows // TILE
    me = lax.axis_index("dap")
    length = len_ref[0]
    first_row = pl.multiple_of(me * rows, TILE)

    def peer(offset):
        return lax.rem(me + offset, groups)

    barrier = pltpu.get_barrier_semaphore()
    for offset in range(1, groups):
        pl.semaphore_signal(barrier, inc=1, device_id={"dap": peer(offset)}, device_id_type=MESH)
    pl.semaphore_wait(barrier, groups - 1)

    lane_head = lax.broadcasted_iota(jnp.int32, (1, width), 1) // head_size
    head_masks = [(lane_head == h).astype(F32).astype(BF16) for h in range(heads)]

    def bias_rows(index, normed, which):
        values = dot_nt(wbias_ref[which], normed)
        for part in range(extent // 128):
            half = values[:8, part * 128 : (part + 1) * 128]
            brow[part, pl.ds(pl.multiple_of(index * 8, 8), 8), :] = half

    def bias_copy(offset, which):
        src = (bsend1, bsend2)[which]
        dst = (bfull1, bfull2)[which]
        return pltpu.make_async_remote_copy(
            src_ref=src,
            dst_ref=dst.at[:, pl.ds(first_row, rows), :],
            send_sem=bias_send.at[which, offset],
            recv_sem=bias_recv.at[which, offset],
            device_id={"dap": peer(offset)},
            device_id_type=MESH,
        )

    def bias_start(which):
        src = (bsend1, bsend2)[which]
        dst = (bfull1, bfull2)[which]
        for h in range(heads):
            halves = [brow[part, pl.ds(h, rows, stride=8), :] for part in range(extent // 128)]
            piece = jnp.concatenate(halves, axis=1).astype(BF16)
            src[h] = piece
            dst[h, pl.ds(first_row, rows), :] = piece
        for offset in range(1, groups):
            bias_copy(offset, which).start()

    def bias_finish(which):
        for offset in range(1, groups):
            bias_copy(offset, which).wait()
        dst = (bfull1, bfull2)[which]
        live = lax.broadcasted_iota(jnp.int32, (1, extent), 1) < length
        for h in range(heads):
            wide = dst[h].astype(F32)
            if which == 1:
                wide = wide.T
            bias_ref[h] = jnp.where(live, wide * LOG2E, -1000000000.0)

    def attend(x, normed, which):
        projected = dot_nn(normed, proj_ref[which])
        factor = LOG2E / math.sqrt(head_size)
        query = (projected[:, :width] * factor).astype(BF16)
        keyed = projected[:, width : 2 * width].astype(BF16)
        valued = projected[:, 2 * width : 3 * width].astype(BF16)
        gate = 1.0 + jnp.exp(-projected[:, 3 * width :])
        ones = [jnp.broadcast_to(head_masks[h], (extent, width)) for h in range(heads)]
        gated = []
        for start in range(0, x.shape[0], extent):
            span = slice(start, start + extent)
            probs = []
            wide_values = []
            for h in range(heads):
                logits = dot_nt(query[span] * head_masks[h], keyed[span]) + bias_ref[h]
                top = jnp.max(logits, axis=-1, keepdims=True)
                probs.append(jnp.exp2(logits - top).astype(BF16))
                wide_values.append(jnp.concatenate([valued[span] * head_masks[h], ones[h]], axis=1))
            mixed = dot_nn(jnp.concatenate(probs, axis=1), jnp.concatenate(wide_values, axis=0))
            gated.append((mixed[:, :width] / (mixed[:, width:] * gate[span])).astype(BF16))
        return x + dot_nn(jnp.concatenate(gated, axis=0), wout_ref[which])

    def transition(x):
        hidden = jnp.maximum(dot_nn(layer_norm(x, tgain_ref[...]), up_ref[...]), 0.0)
        return x + dot_nn(hidden.astype(BF16), down_ref[...])

    def piece_copy(block, offset, phase):
        to = pl.multiple_of(peer(offset) * rows, TILE)
        src = (stage1, stage2)[phase]
        dst = (x2_ref, out_ref)[phase]
        local = src.at[pl.ds(to, rows), pl.ds(pl.multiple_of(block * TILE, TILE), TILE), :]
        place = dst.at[:, pl.ds(pl.multiple_of(first_row + block * TILE, TILE), TILE), :]
        if offset == 0:
            return pltpu.make_async_copy(local, place, own_sem.at[phase, block])
        return pltpu.make_async_remote_copy(
            src_ref=local,
            dst_ref=place,
            send_sem=(one_send, two_send)[phase].at[block, offset],
            recv_sem=(one_recv, two_recv)[phase].at[block, offset],
            device_id={"dap": peer(offset)},
            device_id_type=MESH,
        )

    def send_block(block, phase):
        stage = (stage1, stage2)[phase]
        turned = turn[...].reshape(extent, TILE, width).astype(BF16)
        stage[:, pl.ds(pl.multiple_of(block * TILE, TILE), TILE), :] = turned
        for offset in list(range(1, groups)) + [0]:
            piece_copy(block, offset, phase).start()

    def finish_blocks(phase):
        def body(block, carry):
            for offset in range(groups):
                piece_copy(block, offset, phase).wait()
            return carry

        lax.fori_loop(0, blocks, body, 0)

    def bias_body(step, carry):
        for part in range(UNROLL):
            index = step * UNROLL + part
            normed = layer_norm(pair_ref[index].astype(F32), gain_ref[0:1])
            norm_ref[index] = normed
            bias_rows(index, normed, 0)
        return carry

    lax.fori_loop(0, rows // UNROLL, bias_body, 0)
    bias_start(0)
    bias_finish(0)

    def one_block(block, carry):
        def one_body(step, inner):
            local = step * UNROLL
            index = block * TILE + local
            x = pair_ref[pl.ds(index, UNROLL)].reshape(UNROLL * extent, width).astype(F32)
            normed = norm_ref[pl.ds(index, UNROLL)].reshape(UNROLL * extent, width)
            first = attend(x, normed, 0)
            renormed = layer_norm(first.astype(BF16).astype(F32), gain_ref[1:2])
            for part in range(UNROLL):
                span = slice(part * extent, (part + 1) * extent)
                turn[pl.ds(local + part, extent, stride=TILE), :] = first[span]
                bias_rows(index + part, renormed[span], 1)
            return inner

        lax.fori_loop(0, TILE // UNROLL, one_body, 0)
        send_block(block, 0)
        return carry

    lax.fori_loop(0, blocks, one_block, 0)
    bias_start(1)
    finish_blocks(0)
    bias_finish(1)

    row_live = lax.broadcasted_iota(jnp.int32, (extent, width), 0) < length

    def two_block(block, carry):
        def two_body(step, inner):
            local = step * UNROLL
            index = block * TILE + local
            x = x2_ref[pl.ds(index, UNROLL)].reshape(UNROLL * extent, width).astype(F32)
            second = attend(x, layer_norm(x, gain_ref[1:2]), 1)
            third = transition(second.astype(BF16).astype(F32))
            for part in range(UNROLL):
                limit = jnp.where(first_row + index + part < length, 1.0, 0.0)
                piece = third[part * extent : (part + 1) * extent] * limit
                turn[pl.ds(local + part, extent, stride=TILE), :] = jnp.where(row_live, piece, 0.0)
            return inner

        lax.fori_loop(0, TILE // UNROLL, two_body, 0)
        send_block(block, 1)
        return carry

    lax.fori_loop(0, blocks, two_block, 0)
    finish_blocks(1)


def on_device(
    pair, lengths, attn_gain, attn_proj, attn_bias, attn_out, trans_gain, trans_up, trans_down
):
    current = pair[0]
    rows, extent, width = current.shape
    heads = attn_bias.shape[2]
    groups = lax.axis_size("dap")
    blocks = rows // TILE
    wbias = jnp.pad(jnp.swapaxes(attn_bias, 1, 2), ((0, 0), (0, 16 - heads), (0, 0)))
    vmem = pl.BlockSpec(memory_space=pltpu.VMEM)
    dma = pltpu.SemaphoreType.DMA
    result = pl.pallas_call(
        functools.partial(kernel, groups, heads),
        out_shape=jax.ShapeDtypeStruct(current.shape, BF16),
        in_specs=[vmem, pl.BlockSpec(memory_space=pltpu.SMEM)] + [vmem] * 7,
        out_specs=pl.BlockSpec(memory_space=pl.ANY),
        scratch_shapes=[
            pltpu.VMEM((rows, extent, width), BF16),
            pltpu.VMEM((rows, extent, width), BF16),
            pltpu.VMEM((extent, rows, width), BF16),
            pltpu.VMEM((extent, rows, width), BF16),
            pltpu.VMEM((extent // 128, rows * 8, 128), F32),
            pltpu.VMEM((heads, rows, extent), BF16),
            pltpu.VMEM((heads, rows, extent), BF16),
            pltpu.VMEM((heads, extent, extent), BF16),
            pltpu.VMEM((heads, extent, extent), BF16),
            pltpu.VMEM((heads, extent, extent), F32),
            pltpu.VMEM((extent * TILE, width), F32),
            dma((2, groups)),
            dma((2, groups)),
            dma((blocks, groups)),
            dma((blocks, groups)),
            dma((blocks, groups)),
            dma((blocks, groups)),
            dma((2, blocks)),
        ],
        compiler_params=pltpu.CompilerParams(
            collective_id=0, has_side_effects=True, vmem_limit_bytes=56 * 1024 * 1024
        ),
        cost_estimate=pl.CostEstimate(
            flops=20 * 1000**3, bytes_accessed=16 * 1000**2, transcendentals=40 * 1000**2
        ),
    )(current, lengths, attn_gain, attn_proj, wbias, attn_out, trans_gain[None], trans_up, trans_down)
    return result[None]


def solution(mesh):
    in_specs = (
        P(("parts", "design"), "dap", None, None),
        P(("parts", "design")),
        P(),
        P(),
        P(),
        P(),
        P(),
        P(),
        P(),
    )
    out_specs = P(("parts", "design"), "dap", None, None)
    return jax.shard_map(
        on_device, mesh=mesh, in_specs=in_specs, out_specs=out_specs, check_vma=False
    )
```
